32 devices in a mesh: groups: 2 (over x), train: 16 (over z, y, core).
Axes of the slice: x: 2, y: 2, z: 4, core: 2. Of those that a mesh axis runs over, the one named last changes fastest.
Arguments:
- train_grads: bfloat16 [4, 20480, 4096], P(None, ('groups', 'train')), parts along dimension 1, may hold values from -300 to 300
- token_counts: int32 [20480], P(('groups', 'train')), parts along dimension 0, may hold values from 64 to 511
- queries: bfloat16 [4, 128, 4096], P(None, ('groups', 'train')), parts along dimension 1, may hold values from -6 to 6
- basis_out: float32 [4, 64, 64], replicated, may hold values from -0.75 to 0.75
- basis_in: float32 [4, 64, 64], replicated, may hold values from -0.75 to 0.75
- eig_out: float32 [4, 64], replicated, may hold values from 0.3 to 3
- eig_in: float32 [4, 64], replicated, may hold values from 0.3 to 3
Outputs:
- influence: float32 [20480, 64], P(('groups', 'train')), parts along dimension 0
The draws below stay inside these ranges and needn't reach their ends.
There are 2 independent parts, one for each index of `groups`. The reference program is written for one: setup_inputs(seed, part) draws one part's arguments, and reference() takes and returns one part's arrays. A program takes and returns all parts, laid end to end along the dimension named above; an argument that names none is the same for every part. Nothing has to cross between parts.
All inputs are finite; a program needn't handle non-finite values.
Results may differ from the reference program's by a relative error of at most 0.003.
Values may be sent and summed in bfloat16 or wider, within the bound.
A program may use at most 128 MiB of HBM per device.

```python
import math
import jax
import jax.numpy as jnp
from jax import lax

P_SIZE = 64
PROJ = 4096
LAYERS = 4
QUERIES = 64
ROWS = 10240


def draw_train_grads(key, part):
    key = jax.random.fold_in(key, 11)
    first, second, third = jax.random.split(key, 3)
    noise = jnp.clip(jax.random.normal(first, (LAYERS, ROWS, PROJ), jnp.float32), -5.0, 5.0)
    scale = jnp.exp(jax.random.uniform(second, (ROWS,), jnp.float32, 0.0, math.log(10.0)))
    common = jnp.clip(jax.random.normal(third, (LAYERS, 1, PROJ), jnp.float32), -4.0, 4.0)
    rising = 1.0 + 2.0 * jnp.arange(ROWS, dtype=jnp.float32) / ROWS
    values = 1.5 * scale[None, :, None] * (noise + 0.6 * rising[None, :, None] * common)
    return values.astype(jnp.bfloat16)


def with_ends(result, stream_key, low, high):
    longest = result.shape.index(max(result.shape))
    spots = []
    for shift in (0, 1):
        where = [jax.random.randint(jax.random.fold_in(stream_key, axis), (), 0, length) for axis, length in enumerate(result.shape)]
        where[longest] = (where[longest] + shift) % result.shape[longest]
        spots.append(tuple(where))
    return result.at[spots[0]].set(low).at[spots[1]].set(high)


def shard_levels(rng, extent, cuts, low, high):
    factor_of, own = 1.0, jax.random.fold_in(rng, 6)
    for axis_at, shards_of in cuts:
        draws = jnp.exp(jax.random.uniform(jax.random.fold_in(own, axis_at), (shards_of,), jnp.float32, low / len(cuts), high / len(cuts)))
        factor_of = factor_of * jnp.repeat(draws, extent[axis_at] // shards_of).reshape([-1 if axis == axis_at else 1 for axis in range(len(extent))])
    return factor_of


def centred(key, dims, scale, limit, pieces=(), held_as=jnp.bfloat16):
    entries = scale * jax.random.normal(key, dims, jnp.float32)
    if pieces:
        entries = entries * shard_levels(key, dims, pieces, -0.22, 0.18)
    return jnp.clip(entries, -limit, limit).astype(held_as)


def setup_inputs(seed: int = 0, part: int = 0) -> dict:
    keys = jax.random.split(jax.random.key(seed), 8)
    part_splits = jax.random.split(jax.random.fold_in(keys[7], part), 8)
    train_grads = draw_train_grads(jax.random.fold_in(jax.random.fold_in(keys[7], part), 71), part)
    token_counts = with_ends(jax.random.randint(part_splits[1], (ROWS,), 64, 512), jax.random.fold_in(part_splits[1], 1), 64, 511).astype(jnp.int32)
    queries = centred(part_splits[2], (LAYERS, QUERIES, PROJ), 1.0, 6.0, ((1, 16),))
    basis_out = centred(keys[3], (LAYERS, P_SIZE, P_SIZE), P_SIZE ** -0.5, 0.75, (), jnp.float32)
    basis_in = centred(keys[4], (LAYERS, P_SIZE, P_SIZE), P_SIZE ** -0.5, 0.75, (), jnp.float32)
    eig_out = jnp.clip(jnp.exp(jax.random.uniform(keys[5], (LAYERS, P_SIZE), jnp.float32, math.log(0.3), math.log(3.0))), 0.3, 3.0)
    eig_in = jnp.clip(jnp.exp(jax.random.uniform(keys[6], (LAYERS, P_SIZE), jnp.float32, math.log(0.3), math.log(3.0))), 0.3, 3.0)
    return dict(train_grads=train_grads, token_counts=token_counts, queries=queries, basis_out=basis_out, basis_in=basis_in, eig_out=eig_out, eig_in=eig_in)


def precondition(raw, basis_out, basis_in, eig_out, eig_in):
    width = basis_out.shape[0]
    field = raw.astype(jnp.float32).reshape(raw.shape[0], width, width)
    rotated = jnp.einsum("ji,njk->nik", basis_out, field, precision=lax.Precision.HIGHEST)
    rotated = jnp.einsum("nik,kl->nil", rotated, basis_in, precision=lax.Precision.HIGHEST)
    spectrum = eig_out[:, None] * eig_in[None, :] + 0.01
    scaled = rotated / spectrum
    back = jnp.einsum("ij,njk->nik", basis_out, scaled, precision=lax.Precision.HIGHEST)
    back = jnp.einsum("nik,lk->nil", back, basis_in, precision=lax.Precision.HIGHEST)
    return back.reshape(raw.shape[0], width * width).astype(jnp.bfloat16)


def reference(train_grads, token_counts, queries, basis_out, basis_in, eig_out, eig_in):
    total = jnp.zeros((ROWS, QUERIES), jnp.float32)
    for layer in range(LAYERS):
        conditioned = precondition(queries[layer], basis_out[layer], basis_in[layer], eig_out[layer], eig_in[layer])
        total = total + lax.dot_general(train_grads[layer], conditioned, (((1,), (1,)), ((), ())), preferred_element_type=jnp.float32)
    scores = total / token_counts.astype(jnp.float32)[:, None]
    column_mean = jnp.sum(scores, axis=0) / ROWS
    return scores - column_mean[None, :]
```

```python
import jax
import jax.numpy as jnp
from jax import lax
from jax.sharding import PartitionSpec as P


def precondition(raw, basis_out, basis_in, eig_out, eig_in):
    layers, count, proj = raw.shape
    width = basis_out.shape[1]
    hi = lax.Precision.HIGHEST
    field = raw.astype(jnp.float32).reshape(layers, count, width, width)
    rotated = jnp.einsum("lnjk,lkm->lnjm", field, basis_in, precision=hi)
    rotated = jnp.einsum("lji,lnjm->lnim", basis_out, rotated, precision=hi)
    spectrum = eig_out[:, :, None] * eig_in[:, None, :] + 0.01
    scaled = rotated / spectrum[:, None]
    back = jnp.einsum("lnjk,lmk->lnjm", scaled, basis_in, precision=hi)
    back = jnp.einsum("lij,lnjm->lnim", basis_out, back, precision=hi)
    return back.reshape(layers, count, proj).astype(jnp.bfloat16)


def per_device(train_grads, token_counts, queries, basis_out, basis_in, eig_out, eig_in):
    mine = precondition(queries, basis_out, basis_in, eig_out, eig_in)
    everyone = lax.all_gather(mine, "train", axis=1, tiled=True)
    total = jnp.zeros((train_grads.shape[1], everyone.shape[1]), jnp.float32)
    for layer in range(train_grads.shape[0]):
        total = total + lax.dot_general(
            train_grads[layer], everyone[layer], (((1,), (1,)), ((), ())),
            preferred_element_type=jnp.float32,
        )
    scores = total / token_counts.astype(jnp.float32)[:, None]
    summed = lax.psum(jnp.sum(scores, axis=0), "train")
    column_mean = summed / (scores.shape[0] * lax.axis_size("train"))
    return scores - column_mean[None, :]


def solution(mesh):
    rows = P(None, ("groups", "train"), None)
    in_specs = (rows, P(("groups", "train")), rows, P(), P(), P(), P())
    return jax.shard_map(
        per_device, mesh=mesh, in_specs=in_specs,
        out_specs=P(("groups", "train"), None), check_vma=False,
    )
```

```python
import functools

import jax
import jax.numpy as jnp
from jax import lax
from jax.experimental import pallas as pl
from jax.experimental.pallas import tpu as pltpu
from jax.sharding import PartitionSpec as P

CHUNKS = 4
HIGHEST = lax.Precision.HIGHEST


def precondition(raw, basis_out, basis_in, eig_out, eig_in):
    layers, count, proj = raw.shape
    width = basis_out.shape[1]
    field = raw.astype(jnp.float32).reshape(layers, count, width, width)
    rotated = jnp.einsum("lnjk,lkm->lnjm", field, basis_in, precision=HIGHEST)
    rotated = jnp.einsum("lji,lnjm->lnim", basis_out, rotated, precision=HIGHEST)
    spectrum = eig_out[:, :, None] * eig_in[:, None, :] + 0.01
    scaled = rotated / spectrum[:, None]
    back = jnp.einsum("lnjk,lmk->lnjm", scaled, basis_in, precision=HIGHEST)
    back = jnp.einsum("lij,lnjm->lnim", basis_out, back, precision=HIGHEST)
    return back.reshape(layers, count, proj).astype(jnp.bfloat16)


def plain(train_grads, token_counts, queries, basis_out, basis_in, eig_out, eig_in):
    mine = precondition(queries, basis_out, basis_in, eig_out, eig_in)
    everyone = lax.all_gather(mine, "train", axis=1, tiled=True)
    total = jnp.zeros((train_grads.shape[1], everyone.shape[1]), jnp.float32)
    for layer in range(train_grads.shape[0]):
        total = total + lax.dot_general(
            train_grads[layer], everyone[layer], (((1,), (1,)), ((), ())),
            preferred_element_type=jnp.float32,
        )
    scores = total / token_counts.astype(jnp.float32)[:, None]
    summed = lax.psum(jnp.sum(scores, axis=0), "train")
    column_mean = summed / (scores.shape[0] * lax.axis_size("train"))
    return scores - column_mean[None, :]


def kernel(
    devices, layers, mine_ref, counts_ref, train_ref, out_ref,
    held, rows_of, sums, load_sem, send_sem, recv_sem, sum_send, sum_recv,
):
    me = lax.axis_index("train")
    depth = devices // 4
    z, y, core = me // 4, (me // 2) % 2, me % 2
    local, proj = mine_ref.shape
    wide = proj // CHUNKS
    count = local // layers

    def slot(zz, yy, cc):
        return (zz * 2 + yy) * 2 + cc

    barrier = pltpu.get_barrier_semaphore()
    for step in range(1, devices):
        pl.semaphore_signal(
            barrier, inc=1, device_id={"train": (me + step) % devices},
            device_id_type=pl.DeviceIdType.MESH,
        )

    loads = []
    for chunk in range(CHUNKS):
        cols = pl.ds(chunk * wide, wide)
        loads.append([])
        for layer in range(layers):
            copy = pltpu.make_async_copy(
                train_ref.at[layer, :, cols],
                rows_of.at[chunk, :, pl.ds(layer * wide, wide)],
                load_sem.at[chunk, layer],
            )
            copy.start()
            loads[-1].append(copy)

    held[me] = mine_ref[...]
    pl.semaphore_wait(barrier, devices - 1)

    sent = []

    def send(chunk, which, number, target):
        part = held.at[which, :, pl.ds(chunk * wide, wide)]
        copy = pltpu.make_async_remote_copy(
            src_ref=part, dst_ref=part,
            send_sem=send_sem.at[chunk, number], recv_sem=recv_sem.at[chunk, which],
            device_id={"train": target}, device_id_type=pl.DeviceIdType.MESH,
        )
        copy.start()
        sent.append(copy)

    def arrive(chunk, which):
        part = held.at[which, :, pl.ds(chunk * wide, wide)]
        pltpu.make_async_remote_copy(
            src_ref=part, dst_ref=part,
            send_sem=send_sem.at[chunk, 0], recv_sem=recv_sem.at[chunk, which],
            device_id={"train": me}, device_id_type=pl.DeviceIdType.MESH,
        ).wait_recv()

    across = slot(z, 1 - y, core)
    sibling = slot(z, y, 1 - core)
    for chunk in range(CHUNKS):
        for step in range(1, depth):
            send(chunk, me, step - 1, slot((z + step) % depth, y, core))
        send(chunk, me, depth - 1, across)
        send(chunk, me, 2 * depth - 1, sibling)

    def forward(chunk):
        for step in range(1, depth):
            which = slot((z + step) % depth, y, core)
            arrive(chunk, which)
            send(chunk, which, depth - 1 + step, across)
            send(chunk, which, 2 * depth - 1 + step, sibling)
        for step in range(depth):
            which = slot((z + step) % depth, 1 - y, core)
            arrive(chunk, which)
            send(chunk, which, 3 * depth - 1 + step, sibling)

    total_rows = devices * local
    layer_of = (lax.broadcasted_iota(jnp.int32, (total_rows, 128), 0) // count) % layers
    masks = [
        jnp.where(layer_of == layer, 1.0, 0.0).astype(jnp.bfloat16) for layer in range(layers)
    ]

    def contract(chunk):
        for yy in range(2):
            for step in range(depth):
                arrive(chunk, slot((z + step) % depth, (y + yy) % 2, 1 - core))
        for copy in loads[chunk]:
            copy.wait()
        block = held[:, :, pl.ds(chunk * wide, wide)].reshape(total_rows, wide)
        spread = [jnp.concatenate([mask] * (wide // 128), axis=1) for mask in masks]
        right = jnp.concatenate([block * m for m in spread], axis=1)
        return lax.dot_general(
            rows_of[chunk], right, (((1,), (1,)), ((), ())),
            preferred_element_type=jnp.float32,
        )

    forward(0)
    total = None
    for chunk in range(CHUNKS):
        if chunk + 1 < CHUNKS:
            forward(chunk + 1)
        part = contract(chunk)
        total = part if total is None else total + part

    scores = total / counts_ref[...].astype(jnp.float32)
    sums[me] = jnp.sum(scores, axis=0, keepdims=True)
    told = []
    for step in range(1, devices):
        copy = pltpu.make_async_remote_copy(
            src_ref=sums.at[me], dst_ref=sums.at[me],
            send_sem=sum_send.at[step], recv_sem=sum_recv.at[me],
            device_id={"train": (me + step) % devices}, device_id_type=pl.DeviceIdType.MESH,
        )
        copy.start()
        told.append(copy)

    queries = devices * count
    source = lax.broadcasted_iota(jnp.int32, (total_rows, queries), 0)
    column = lax.broadcasted_iota(jnp.int32, (total_rows, queries), 1)
    pick = (source // local) * count + source % count == column
    pick = jnp.where(pick, 1.0, 0.0)
    scores = jnp.dot(scores, pick, precision=HIGHEST, preferred_element_type=jnp.float32)
    for step in range(1, devices):
        which = (me + step) % devices
        pltpu.make_async_remote_copy(
            src_ref=sums.at[which], dst_ref=sums.at[which],
            send_sem=sum_send.at[0], recv_sem=sum_recv.at[which],
            device_id={"train": me}, device_id_type=pl.DeviceIdType.MESH,
        ).wait_recv()
    summed = sums[0]
    for which in range(1, devices):
        summed = summed + sums[which]
    mean = summed * (1.0 / (devices * scores.shape[0]))
    mean = jnp.broadcast_to(mean, (8, total_rows))
    mean = jnp.dot(mean, pick, precision=HIGHEST, preferred_element_type=jnp.float32)
    out_ref[...] = scores - mean[0:1]
    for copy in sent + told:
        copy.wait_send()


def fused(train_grads, token_counts, queries, basis_out, basis_in, eig_out, eig_in):
    layers, rows, proj = train_grads.shape
    devices = lax.axis_size("train")
    count = queries.shape[1]
    mine = precondition(queries, basis_out, basis_in, eig_out, eig_in)
    mine = mine.reshape(layers * count, proj)
    local = layers * count
    wide = proj // CHUNKS
    vmem = pl.BlockSpec(memory_space=pltpu.VMEM)
    return pl.pallas_call(
        functools.partial(kernel, devices, layers),
        out_shape=jax.ShapeDtypeStruct((rows, devices * count), jnp.float32),
        in_specs=[vmem, vmem, pl.BlockSpec(memory_space=pl.ANY)],
        out_specs=vmem,
        scratch_shapes=[
            pltpu.VMEM((devices, local, proj), jnp.bfloat16),
            pltpu.VMEM((CHUNKS, rows, layers * wide), jnp.bfloat16),
            pltpu.VMEM((devices, 1, devices * local), jnp.float32),
            pltpu.SemaphoreType.DMA((CHUNKS, layers)),
            pltpu.SemaphoreType.DMA((CHUNKS, devices)),
            pltpu.SemaphoreType.DMA((CHUNKS, devices)),
            pltpu.SemaphoreType.DMA((devices,)),
            pltpu.SemaphoreType.DMA((devices,)),
        ],
        compiler_params=pltpu.CompilerParams(
            collective_id=0, has_side_effects=True, vmem_limit_bytes=56 * 2**20
        ),
        cost_estimate=pl.CostEstimate(
            flops=2 * rows * layers * proj * devices * count,
            bytes_accessed=layers * rows * proj * 2, transcendentals=0,
        ),
    )(mine, token_counts.reshape(rows, 1), train_grads)


def solution(mesh):
    devices = mesh.shape["train"]

    def per_device(train_grads, token_counts, queries, *factors):
        layers, rows, proj = train_grads.shape
        local = layers * queries.shape[1]
        fits = devices % 4 == 0 and local % 16 == 0 and proj % (128 * CHUNKS) == 0
        fits = fits and devices * local <= 512 and rows % 16 == 0
        fits = fits and layers * rows * proj <= 12 * 2**20
        body = fused if fits else plain
        return body(train_grads, token_counts, queries, *factors)

    rows = P(None, ("groups", "train"), None)
    in_specs = (rows, P(("groups", "train")), rows, P(), P(), P(), P())
    return jax.shard_map(
        per_device, mesh=mesh, in_specs=in_specs,
        out_specs=P(("groups", "train"), None), check_vma=False,
    )
```

```python
import functools

import jax
import jax.numpy as jnp
from jax import lax
from jax.experimental import pallas as pl
from jax.experimental.pallas import tpu as pltpu
from jax.sharding import PartitionSpec as P

CHUNKS = 2
HIGHEST = lax.Precision.HIGHEST


def precondition(raw, basis_out, basis_in, eig_out, eig_in):
    layers, count, proj = raw.shape
    width = basis_out.shape[1]
    field = raw.astype(jnp.float32).reshape(layers, count, width, width)
    rotated = jnp.einsum("lnjk,lkm->lnjm", field, basis_in, precision=HIGHEST)
    rotated = jnp.einsum("lji,lnjm->lnim", basis_out, rotated, precision=HIGHEST)
    spectrum = eig_out[:, :, None] * eig_in[:, None, :] + 0.01
    scaled = rotated / spectrum[:, None]
    back = jnp.einsum("lnjk,lmk->lnjm", scaled, basis_in, precision=HIGHEST)
    back = jnp.einsum("lij,lnjm->lnim", basis_out, back, precision=HIGHEST)
    return back.reshape(layers, count, proj).astype(jnp.bfloat16)


def plain(train_grads, token_counts, queries, basis_out, basis_in, eig_out, eig_in):
    mine = precondition(queries, basis_out, basis_in, eig_out, eig_in)
    everyone = lax.all_gather(mine, "train", axis=1, tiled=True)
    total = jnp.zeros((train_grads.shape[1], everyone.shape[1]), jnp.float32)
    for layer in range(train_grads.shape[0]):
        total = total + lax.dot_general(
            train_grads[layer], everyone[layer], (((1,), (1,)), ((), ())),
            preferred_element_type=jnp.float32,
        )
    scores = total / token_counts.astype(jnp.float32)[:, None]
    summed = lax.psum(jnp.sum(scores, axis=0), "train")
    column_mean = summed / (scores.shape[0] * lax.axis_size("train"))
    return scores - column_mean[None, :]


def column_of(row):
    parts = []
    for start in range(0, row.shape[1], 128):
        piece = row[:, start : start + 128]
        size = piece.shape[1]
        down = lax.broadcasted_iota(jnp.int32, (size, size), 0)
        along = lax.broadcasted_iota(jnp.int32, (size, size), 1)
        spread = jnp.where(down == along, jnp.broadcast_to(piece, (size, size)), 0.0)
        parts.append(jnp.sum(spread, axis=1, keepdims=True))
    return parts[0] if len(parts) == 1 else jnp.concatenate(parts, axis=0)


def dot(a, b, over_a=1, over_b=0):
    return lax.dot_general(
        a, b, (((over_a,), (over_b,)), ((), ())),
        precision=HIGHEST, preferred_element_type=jnp.float32,
    )


def condition_into(
    mine, field, raw_ref, basis_out_ref, basis_in_ref, eig_out_ref, eig_in_ref
):
    layers, count, proj = raw_ref.shape
    width = basis_out_ref.shape[1]
    pairs, lanes = width // 2, 2 * width
    for layer in range(layers):
        raw = raw_ref[layer].astype(jnp.float32)
        for k in range(pairs):
            field[layer * count : (layer + 1) * count, k, :] = raw[:, k * lanes : (k + 1) * lanes]
    new = lax.broadcasted_iota(jnp.int32, (width, width), 0)
    old = lax.broadcasted_iota(jnp.int32, (width, width), 1)
    order = jnp.where(2 * (new % pairs) + new // pairs == old, 1.0, 0.0)
    half = lax.broadcasted_iota(jnp.int32, (lanes, lanes), 0) // width
    other = lax.broadcasted_iota(jnp.int32, (lanes, lanes), 1) // width
    for layer in range(layers):
        block = field[layer * count : (layer + 1) * count].reshape(count * pairs, lanes)
        basis = basis_in_ref[layer]
        twice = jnp.concatenate([basis, basis], axis=1)
        twice = jnp.where(half == other, jnp.concatenate([twice, twice], axis=0), 0.0)
        left = dot(order, basis_out_ref[layer])
        turned = dot(block, twice)
        rows = [turned[q * pairs : (q + 1) * pairs] for q in range(count)]
        even = jnp.concatenate([r[:, :width] for r in rows], axis=1)
        odd = jnp.concatenate([r[:, width:] for r in rows], axis=1)
        rotated = dot(left, jnp.concatenate([even, odd], axis=0), 0, 0)
        wide = jnp.concatenate([eig_in_ref[layer : layer + 1, :]] * count, axis=1)
        scaled = rotated / (column_of(eig_out_ref[layer : layer + 1, :]) * wide + 0.01)
        back = dot(left, scaled)
        rows = [
            jnp.concatenate(
                [back[:pairs, q * width : (q + 1) * width], back[pairs:, q * width : (q + 1) * width]],
                axis=1,
            )
            for q in range(count)
        ]
        done = dot(jnp.concatenate(rows, axis=0), twice, 1, 1)
        field[layer * count : (layer + 1) * count] = done.reshape(count, pairs, lanes)
    for k in range(pairs):
        mine[:, k * lanes : (k + 1) * lanes] = field[:, k, :].astype(jnp.bfloat16)


def kernel(
    devices, layers, raw_ref, counts_ref, basis_out_ref, basis_in_ref, eig_out_ref, eig_in_ref,
    train_ref, out_ref, held, rows_of, sums, field, load_sem, send_sem, recv_sem, sum_send, sum_recv,
):
    me = lax.axis_index("train")
    depth = devices // 4
    z, y, core = me // 4, (me // 2) % 2, me % 2
    count, proj = raw_ref.shape[1:]
    local = layers * count
    wide = proj // CHUNKS

    def slot(zz, yy, cc):
        return (zz * 2 + yy) * 2 + cc

    barrier = pltpu.get_barrier_semaphore()
    for step in range(1, devices):
        pl.semaphore_signal(
            barrier, inc=1, device_id={"train": (me + step) % devices},
            device_id_type=pl.DeviceIdType.MESH,
        )

    loads = []
    for chunk in range(CHUNKS):
        cols = pl.ds(chunk * wide, wide)
        loads.append([])
        for layer in range(layers):
            copy = pltpu.make_async_copy(
                train_ref.at[layer, :, cols],
                rows_of.at[chunk, :, pl.ds(layer * wide, wide)],
                load_sem.at[chunk, layer],
            )
            copy.start()
            loads[-1].append(copy)

    condition_into(
        held.at[me], field, raw_ref, basis_out_ref, basis_in_ref, eig_out_ref, eig_in_ref
    )
    inverse = column_of(1.0 / counts_ref[...].astype(jnp.float32))
    pl.semaphore_wait(barrier, devices - 1)

    sent = []

    def send(chunk, which, number, target):
        part = held.at[which, :, pl.ds(chunk * wide, wide)]
        copy = pltpu.make_async_remote_copy(
            src_ref=part, dst_ref=part,
            send_sem=send_sem.at[chunk, number], recv_sem=recv_sem.at[chunk, which],
            device_id={"train": target}, device_id_type=pl.DeviceIdType.MESH,
        )
        copy.start()
        sent.append(copy)

    def arrive(chunk, which):
        part = held.at[which, :, pl.ds(chunk * wide, wide)]
        pltpu.make_async_remote_copy(
            src_ref=part, dst_ref=part,
            send_sem=send_sem.at[chunk, 0], recv_sem=recv_sem.at[chunk, which],
            device_id={"train": me}, device_id_type=pl.DeviceIdType.MESH,
        ).wait_recv()

    across = slot(z, 1 - y, core)
    sibling = slot(z, y, 1 - core)
    for chunk in range(CHUNKS):
        for step in range(1, depth):
            send(chunk, me, step - 1, slot((z + step) % depth, y, core))
        send(chunk, me, depth - 1, across)
        send(chunk, me, 2 * depth - 1, sibling)

    def forward(chunk):
        for step in range(1, depth):
            which = slot((z + step) % depth, y, core)
            arrive(chunk, which)
            send(chunk, which, depth - 1 + step, across)
            send(chunk, which, 2 * depth - 1 + step, sibling)
        for step in range(depth):
            which = slot((z + step) % depth, 1 - y, core)
            arrive(chunk, which)
            send(chunk, which, 3 * depth - 1 + step, sibling)

    total_rows = devices * local
    layer_of = (lax.broadcasted_iota(jnp.int32, (total_rows, 128), 0) // count) % layers
    masks = [
        jnp.where(layer_of == layer, 1.0, 0.0).astype(jnp.bfloat16) for layer in range(layers)
    ]

    def contract(chunk):
        for yy in range(2):
            for step in range(depth):
                arrive(chunk, slot((z + step) % depth, (y + yy) % 2, 1 - core))
        for copy in loads[chunk]:
            copy.wait()
        block = held[:, :, pl.ds(chunk * wide, wide)].reshape(total_rows, wide)
        spread = [jnp.concatenate([mask] * (wide // 128), axis=1) for mask in masks]
        right = jnp.concatenate([block * m for m in spread], axis=1)
        return lax.dot_general(
            rows_of[chunk], right, (((1,), (1,)), ((), ())),
            preferred_element_type=jnp.float32,
        )

    forward(0)
    total = None
    for chunk in range(CHUNKS):
        if chunk + 1 < CHUNKS:
            forward(chunk + 1)
        part = contract(chunk)
        total = part if total is None else total + part

    scores = total * inverse
    sums[me] = jnp.sum(scores, axis=0, keepdims=True)
    told = []
    for step in range(1, devices):
        copy = pltpu.make_async_remote_copy(
            src_ref=sums.at[me], dst_ref=sums.at[me],
            send_sem=sum_send.at[step], recv_sem=sum_recv.at[me],
            device_id={"train": (me + step) % devices}, device_id_type=pl.DeviceIdType.MESH,
        )
        copy.start()
        told.append(copy)

    queries = devices * count
    source = lax.broadcasted_iota(jnp.int32, (queries, total_rows), 1)
    column = lax.broadcasted_iota(jnp.int32, (queries, total_rows), 0)
    pick = (source // local) * count + source % count == column
    flat = lax.dot_general(
        jnp.where(pick, 1.0, 0.0), scores, (((1,), (1,)), ((), ())),
        precision=HIGHEST, preferred_element_type=jnp.float32,
    )
    for step in range(1, devices):
        which = (me + step) % devices
        pltpu.make_async_remote_copy(
            src_ref=sums.at[which], dst_ref=sums.at[which],
            send_sem=sum_send.at[0], recv_sem=sum_recv.at[which],
            device_id={"train": me}, device_id_type=pl.DeviceIdType.MESH,
        ).wait_recv()
    summed = sums[0]
    for which in range(1, devices):
        summed = summed + sums[which]
    mean = summed * (1.0 / (devices * scores.shape[0]))
    mean = jnp.broadcast_to(mean, (queries, total_rows))
    mean = jnp.sum(jnp.where(pick, mean, 0.0), axis=1, keepdims=True)
    out_ref[...] = flat - mean
    for copy in sent + told:
        copy.wait_send()


def fused(train_grads, token_counts, queries, basis_out, basis_in, eig_out, eig_in):
    layers, rows, proj = train_grads.shape
    devices = lax.axis_size("train")
    count = queries.shape[1]
    local = layers * count
    wide = proj // CHUNKS
    vmem = pl.BlockSpec(memory_space=pltpu.VMEM)
    flat = pl.pallas_call(
        functools.partial(kernel, devices, layers),
        out_shape=jax.ShapeDtypeStruct((devices * count, rows), jnp.float32),
        in_specs=[vmem] * 6 + [pl.BlockSpec(memory_space=pl.ANY)],
        out_specs=vmem,
        scratch_shapes=[
            pltpu.VMEM((devices, local, proj), jnp.bfloat16),
            pltpu.VMEM((CHUNKS, rows, layers * wide), jnp.bfloat16),
            pltpu.VMEM((devices, 1, devices * local), jnp.float32),
            pltpu.VMEM((local, basis_out.shape[1] // 2, 2 * basis_out.shape[1]), jnp.float32),
            pltpu.SemaphoreType.DMA((CHUNKS, layers)),
            pltpu.SemaphoreType.DMA((CHUNKS, devices)),
            pltpu.SemaphoreType.DMA((CHUNKS, devices)),
            pltpu.SemaphoreType.DMA((devices,)),
            pltpu.SemaphoreType.DMA((devices,)),
        ],
        compiler_params=pltpu.CompilerParams(
            collective_id=0, has_side_effects=True, vmem_limit_bytes=56 * 2**20
        ),
        cost_estimate=pl.CostEstimate(
            flops=2 * rows * layers * proj * devices * count,
            bytes_accessed=layers * rows * proj * 2, transcendentals=0,
        ),
    )(
        queries, token_counts.reshape(1, rows), basis_out, basis_in, eig_out, eig_in, train_grads
    )
    return flat.T


def solution(mesh):
    devices = mesh.shape["train"]

    def per_device(train_grads, token_counts, queries, *factors):
        layers, rows, proj = train_grads.shape
        local = layers * queries.shape[1]
        fits = devices % 4 == 0 and local % 16 == 0 and proj % (128 * CHUNKS) == 0
        fits = fits and proj == 4096 and devices * local <= 512 and rows % 16 == 0
        fits = fits and layers * rows * proj <= 12 * 2**20
        body = fused if fits else plain
        return body(train_grads, token_counts, queries, *factors)

    rows = P(None, ("groups", "train"), None)
    in_specs = (rows, P(("groups", "train")), rows, P(), P(), P(), P())
    return jax.shard_map(
        per_device, mesh=mesh, in_specs=in_specs,
        out_specs=P(("groups", "train"), None), check_vma=False,
    )
```

```python
import functools

import jax
import jax.numpy as jnp
from jax import lax
from jax.experimental import pallas as pl
from jax.experimental.pallas import tpu as pltpu
from jax.sharding import PartitionSpec as P

CHUNKS = 2
HIGHEST = lax.Precision.HIGHEST


def precondition(raw, basis_out, basis_in, eig_out, eig_in):
    layers, count, proj = raw.shape
    width = basis_out.shape[1]
    field = raw.astype(jnp.float32).reshape(layers, count, width, width)
    rotated = jnp.einsum("lnjk,lkm->lnjm", field, basis_in, precision=HIGHEST)
    rotated = jnp.einsum("lji,lnjm->lnim", basis_out, rotated, precision=HIGHEST)
    spectrum = eig_out[:, :, None] * eig_in[:, None, :] + 0.01
    scaled = rotated / spectrum[:, None]
    back = jnp.einsum("lnjk,lmk->lnjm", scaled, basis_in, precision=HIGHEST)
    back = jnp.einsum("lij,lnjm->lnim", basis_out, back, precision=HIGHEST)
    return back.reshape(layers, count, proj).astype(jnp.bfloat16)


def plain(train_grads, token_counts, queries, basis_out, basis_in, eig_out, eig_in):
    mine = precondition(queries, basis_out, basis_in, eig_out, eig_in)
    everyone = lax.all_gather(mine, "train", axis=1, tiled=True)
    total = jnp.zeros((train_grads.shape[1], everyone.shape[1]), jnp.float32)
    for layer in range(train_grads.shape[0]):
        total = total + lax.dot_general(
            train_grads[layer], everyone[layer], (((1,), (1,)), ((), ())),
            preferred_element_type=jnp.float32,
        )
    scores = total / token_counts.astype(jnp.float32)[:, None]
    summed = lax.psum(jnp.sum(scores, axis=0), "train")
    column_mean = summed / (scores.shape[0] * lax.axis_size("train"))
    return scores - column_mean[None, :]


def column_of(row):
    parts = []
    for start in range(0, row.shape[1], 128):
        piece = row[:, start : start + 128]
        size = piece.shape[1]
        down = lax.broadcasted_iota(jnp.int32, (size, size), 0)
        along = lax.broadcasted_iota(jnp.int32, (size, size), 1)
        spread = jnp.where(down == along, jnp.broadcast_to(piece, (size, size)), 0.0)
        parts.append(jnp.sum(spread, axis=1, keepdims=True))
    return parts[0] if len(parts) == 1 else jnp.concatenate(parts, axis=0)


def dot(a, b, over_a=1, over_b=0):
    def product(left, right):
        return lax.dot_general(
            left, right, (((over_a,), (over_b,)), ((), ())), preferred_element_type=jnp.float32
        )

    a_high, b_high = a.astype(jnp.bfloat16), b.astype(jnp.bfloat16)
    a_low = (a - a_high.astype(jnp.float32)).astype(jnp.bfloat16)
    b_low = (b - b_high.astype(jnp.float32)).astype(jnp.bfloat16)
    return product(a_high, b_high) + (product(a_high, b_low) + product(a_low, b_high))


def condition_into(
    mine, field, raw_ref, basis_out_ref, basis_in_ref, eig_out_ref, eig_in_ref
):
    layers, count, proj = raw_ref.shape
    width = basis_out_ref.shape[1]
    pairs, lanes = width // 2, 2 * width
    for layer in range(layers):
        raw = raw_ref[layer].astype(jnp.float32)
        for k in range(pairs):
            field[layer * count : (layer + 1) * count, k, :] = raw[:, k * lanes : (k + 1) * lanes]
    new = lax.broadcasted_iota(jnp.int32, (width, width), 0)
    old = lax.broadcasted_iota(jnp.int32, (width, width), 1)
    order = jnp.where(2 * (new % pairs) + new // pairs == old, 1.0, 0.0)
    half = lax.broadcasted_iota(jnp.int32, (lanes, lanes), 0) // width
    other = lax.broadcasted_iota(jnp.int32, (lanes, lanes), 1) // width
    for layer in range(layers):
        block = field[layer * count : (layer + 1) * count].reshape(count * pairs, lanes)
        basis = basis_in_ref[layer]
        twice = jnp.concatenate([basis, basis], axis=1)
        twice = jnp.where(half == other, jnp.concatenate([twice, twice], axis=0), 0.0)
        left = dot(order, basis_out_ref[layer])
        turned = dot(block, twice)
        rows = [turned[q * pairs : (q + 1) * pairs] for q in range(count)]
        even = jnp.concatenate([r[:, :width] for r in rows], axis=1)
        odd = jnp.concatenate([r[:, width:] for r in rows], axis=1)
        rotated = dot(left, jnp.concatenate([even, odd], axis=0), 0, 0)
        wide = jnp.concatenate([eig_in_ref[layer : layer + 1, :]] * count, axis=1)
        scaled = rotated / (column_of(eig_out_ref[layer : layer + 1, :]) * wide + 0.01)
        back = dot(left, scaled)
        rows = [
            jnp.concatenate(
                [back[:pairs, q * width : (q + 1) * width], back[pairs:, q * width : (q + 1) * width]],
                axis=1,
            )
            for q in range(count)
        ]
        done = dot(jnp.concatenate(rows, axis=0), twice, 1, 1)
        field[layer * count : (layer + 1) * count] = done.reshape(count, pairs, lanes)
    for k in range(pairs):
        mine[:, k * lanes : (k + 1) * lanes] = field[:, k, :].astype(jnp.bfloat16)


def kernel(
    devices, layers, raw_ref, counts_ref, basis_out_ref, basis_in_ref, eig_out_ref, eig_in_ref,
    train_ref, out_ref, mean_ref, held, rows_of, sums, field, load_sem, send_sem, recv_sem, sum_send, sum_recv,
):
    me = lax.axis_index("train")
    depth = devices // 4
    z, y, core = me // 4, (me // 2) % 2, me % 2
    count, proj = raw_ref.shape[1:]
    local = layers * count
    wide = proj // CHUNKS

    def slot(zz, yy, cc):
        return (zz * 2 + yy) * 2 + cc

    barrier = pltpu.get_barrier_semaphore()
    for step in range(1, devices):
        pl.semaphore_signal(
            barrier, inc=1, device_id={"train": (me + step) % devices},
            device_id_type=pl.DeviceIdType.MESH,
        )

    loads = []
    for chunk in range(CHUNKS):
        cols = pl.ds(chunk * wide, wide)
        loads.append([])
        for layer in range(layers):
            copy = pltpu.make_async_copy(
                train_ref.at[layer, :, cols],
                rows_of.at[chunk, :, pl.ds(layer * wide, wide)],
                load_sem.at[chunk, layer],
            )
            copy.start()
            loads[-1].append(copy)

    condition_into(
        held.at[me], field, raw_ref, basis_out_ref, basis_in_ref, eig_out_ref, eig_in_ref
    )
    inverse = column_of(1.0 / counts_ref[...].reshape(1, counts_ref.shape[0]).astype(jnp.float32))
    pl.semaphore_wait(barrier, devices - 1)

    sent = []

    def send(chunk, which, number, target):
        part = held.at[which, :, pl.ds(chunk * wide, wide)]
        copy = pltpu.make_async_remote_copy(
            src_ref=part, dst_ref=part,
            send_sem=send_sem.at[chunk, number], recv_sem=recv_sem.at[chunk, which],
            device_id={"train": target}, device_id_type=pl.DeviceIdType.MESH,
        )
        copy.start()
        sent.append(copy)

    def arrive(chunk, which):
        part = held.at[which, :, pl.ds(chunk * wide, wide)]
        pltpu.make_async_remote_copy(
            src_ref=part, dst_ref=part,
            send_sem=send_sem.at[chunk, 0], recv_sem=recv_sem.at[chunk, which],
            device_id={"train": me}, device_id_type=pl.DeviceIdType.MESH,
        ).wait_recv()

    across = slot(z, 1 - y, core)
    sibling = slot(z, y, 1 - core)
    for chunk in range(CHUNKS):
        for step in range(1, depth):
            send(chunk, me, step - 1, slot((z + step) % depth, y, core))
        send(chunk, me, depth - 1, across)
        send(chunk, me, 2 * depth - 1, sibling)

    def forward(chunk):
        for step in range(1, depth):
            which = slot((z + step) % depth, y, core)
            arrive(chunk, which)
            send(chunk, which, depth - 1 + step, across)
            send(chunk, which, 2 * depth - 1 + step, sibling)
        for step in range(depth):
            which = slot((z + step) % depth, 1 - y, core)
            arrive(chunk, which)
            send(chunk, which, 3 * depth - 1 + step, sibling)

    total_rows = devices * local
    layer_of = (lax.broadcasted_iota(jnp.int32, (total_rows, 128), 0) // count) % layers
    masks = [
        jnp.where(layer_of == layer, 1.0, 0.0).astype(jnp.bfloat16) for layer in range(layers)
    ]

    def contract(chunk):
        for yy in range(2):
            for step in range(depth):
                arrive(chunk, slot((z + step) % depth, (y + yy) % 2, 1 - core))
        for copy in loads[chunk]:
            copy.wait()
        block = held[:, :, pl.ds(chunk * wide, wide)].reshape(total_rows, wide)
        spread = [jnp.concatenate([mask] * (wide // 128), axis=1) for mask in masks]
        right = jnp.concatenate([block * m for m in spread], axis=1)
        return lax.dot_general(
            rows_of[chunk], right, (((1,), (1,)), ((), ())),
            preferred_element_type=jnp.float32,
        )

    forward(0)
    total = None
    for chunk in range(CHUNKS):
        if chunk + 1 < CHUNKS:
            forward(chunk + 1)
        part = contract(chunk)
        total = part if total is None else total + part

    scores = total * inverse
    sums[me] = jnp.sum(scores, axis=0, keepdims=True)
    told = []
    for step in range(1, devices):
        copy = pltpu.make_async_remote_copy(
            src_ref=sums.at[me], dst_ref=sums.at[me],
            send_sem=sum_send.at[step], recv_sem=sum_recv.at[me],
            device_id={"train": (me + step) % devices}, device_id_type=pl.DeviceIdType.MESH,
        )
        copy.start()
        told.append(copy)

    queries = devices * count
    source = lax.broadcasted_iota(jnp.int32, (queries, total_rows), 1)
    column = lax.broadcasted_iota(jnp.int32, (queries, total_rows), 0)
    pick = (source // local) * count + source % count == column
    flat = lax.dot_general(
        jnp.where(pick, 1.0, 0.0), scores, (((1,), (1,)), ((), ())),
        precision=HIGHEST, preferred_element_type=jnp.float32,
    )
    out_ref[...] = flat
    for step in range(1, devices):
        which = (me + step) % devices
        pltpu.make_async_remote_copy(
            src_ref=sums.at[which], dst_ref=sums.at[which],
            send_sem=sum_send.at[0], recv_sem=sum_recv.at[which],
            device_id={"train": me}, device_id_type=pl.DeviceIdType.MESH,
        ).wait_recv()
    summed = sums[0]
    for which in range(1, devices):
        summed = summed + sums[which]
    mean = summed * (1.0 / (devices * scores.shape[0]))
    mean = jnp.broadcast_to(mean, (queries, total_rows))
    mean = jnp.sum(jnp.where(pick, mean, 0.0), axis=1, keepdims=True)
    mean_ref[...] = mean
    for copy in sent + told:
        copy.wait_send()


def fused(train_grads, token_counts, queries, basis_out, basis_in, eig_out, eig_in):
    layers, rows, proj = train_grads.shape
    devices = lax.axis_size("train")
    count = queries.shape[1]
    local = layers * count
    wide = proj // CHUNKS
    vmem = pl.BlockSpec(memory_space=pltpu.VMEM)
    flat, mean = pl.pallas_call(
        functools.partial(kernel, devices, layers),
        out_shape=[
            jax.ShapeDtypeStruct((devices * count, rows), jnp.float32),
            jax.ShapeDtypeStruct((devices * count, 1), jnp.float32),
        ],
        in_specs=[vmem] * 6 + [pl.BlockSpec(memory_space=pl.ANY)],
        out_specs=[vmem, vmem],
        scratch_shapes=[
            pltpu.VMEM((devices, local, proj), jnp.bfloat16),
            pltpu.VMEM((CHUNKS, rows, layers * wide), jnp.bfloat16),
            pltpu.VMEM((devices, 1, devices * local), jnp.float32),
            pltpu.VMEM((local, basis_out.shape[1] // 2, 2 * basis_out.shape[1]), jnp.float32),
            pltpu.SemaphoreType.DMA((CHUNKS, layers)),
            pltpu.SemaphoreType.DMA((CHUNKS, devices)),
            pltpu.SemaphoreType.DMA((CHUNKS, devices)),
            pltpu.SemaphoreType.DMA((devices,)),
            pltpu.SemaphoreType.DMA((devices,)),
        ],
        compiler_params=pltpu.CompilerParams(
            collective_id=0, has_side_effects=True, vmem_limit_bytes=56 * 2**20
        ),
        cost_estimate=pl.CostEstimate(
            flops=2 * rows * layers * proj * devices * count,
            bytes_accessed=layers * rows * proj * 2, transcendentals=0,
        ),
    )(
        queries, token_counts, basis_out, basis_in, eig_out, eig_in, train_grads
    )
    return (flat - mean).T


def solution(mesh):
    devices = mesh.shape["train"]

    def per_device(train_grads, token_counts, queries, *factors):
        layers, rows, proj = train_grads.shape
        local = layers * queries.shape[1]
        fits = devices % 4 == 0 and local % 16 == 0 and proj % (128 * CHUNKS) == 0
        fits = fits and proj == 4096 and devices * local <= 512 and rows % 16 == 0
        fits = fits and layers * rows * proj <= 12 * 2**20
        body = fused if fits else plain
        return body(train_grads, token_counts, queries, *factors)

    rows = P(None, ("groups", "train"), None)
    in_specs = (rows, P(("groups", "train")), rows, P(), P(), P(), P())
    return jax.shard_map(
        per_device, mesh=mesh, in_specs=in_specs,
        out_specs=P(("groups", "train"), None), check_vma=False,
    )
```
